32 devices in a mesh: wide: 8 (over z, x), narrow: 4 (over y, core).
Axes of the slice: x: 2, y: 2, z: 4, core: 2. Of those that a mesh axis runs over, the one named last changes fastest.
Arguments:
- treated: bfloat16 [8192, 512], P(('wide', 'narrow')), may hold values from -6 to 6
- control: bfloat16 [8192, 512], P('wide'), may hold values from -6 to 6
- treated_weight: float32 [8192], P(('wide', 'narrow')), may hold values from 0.5 to 2
- control_weight: float32 [8192], replicated, may hold values from 0.5 to 2
- band: int32 [64, 24], P(('wide', 'narrow')), may hold values from 0 to 1, as said below
Outputs:
- grad_treated: float32 [8192, 512], P(('wide', 'narrow'))
- grad_control: float32 [8192, 512], P(('wide', 'narrow'))
The draws below stay inside these ranges and needn't reach their ends.
Inputs may be any that keep to these rules, and one draw needn't show every extreme that they name: band[t, k] = 1 pairs treated block t with control block (t // 8 - 1) * 8 + k. For each t the ones form one run of k that contains k = 8 + t % 8; every k whose control block lies outside 0 to 63 is 0.
All inputs are finite; a program needn't handle non-finite values.
Results may differ from the reference program's by a relative error of at most 0.0055.
Values may be sent and summed in bfloat16 or wider, within the bound.
A program may use at most 64 MiB of HBM per device.

```python
import math
import jax
import jax.numpy as jnp
from jax import lax

REPRESENT_WIDTH = 512
BLOCK = 128
SWEEPS = 2
SB = 8
SLAB = 1024
NT = 8192
NC = 8192
NTB = 64
N_WIDE = 8


def draw_band(key, part):
    key_low, key_high = jax.random.split(key)
    blocks = jnp.arange(NTB, dtype=jnp.int32)
    position = blocks % SB
    reach_low = jax.random.randint(key_low, (NTB,), 0, SB + 1, dtype=jnp.int32)
    reach_high = jax.random.randint(key_high, (NTB,), 0, SB + 1, dtype=jnp.int32)
    columns = jnp.arange(3 * SB, dtype=jnp.int32)
    offset = columns[None, :] - SB - position[:, None]
    target = blocks[:, None] + offset
    allowed = (offset >= -reach_low[:, None]) & (offset <= reach_high[:, None]) & (target >= 0) & (target < NTB)
    return allowed.astype(jnp.int32)


def steps_of(key, shape, cuts, low, high):
    loudness = 1.0
    for axis_at, shards_of in cuts:
        heights = jax.random.uniform(jax.random.fold_in(jax.random.fold_in(key, 6), axis_at), (shards_of,), jnp.float32, low / len(cuts), high / len(cuts))
        loudness = loudness * jnp.repeat(jnp.exp(heights), shape[axis_at] // shards_of).reshape((-1,) + (1,) * (len(shape) - 1 - axis_at))
    return loudness


def noise(own_key, shape, deviation, most, cuts=(), held_as=jnp.bfloat16):
    array = deviation * jax.random.normal(own_key, shape, jnp.float32)
    if cuts:
        array = array * steps_of(own_key, shape, cuts, -0.22, 0.18)
    return jnp.clip(array, -most, most).astype(held_as)


def setup_inputs(seed: int = 0) -> dict:
    key_of = jax.random.split(jax.random.key(seed), 6)
    treated = noise(key_of[0], (NT, REPRESENT_WIDTH), 1.0, 6.0, ((0, 32),))
    control = noise(key_of[1], (NC, REPRESENT_WIDTH), 1.0, 6.0, ((0, 8),))
    treated_weight = jnp.clip(jnp.exp(math.log(2.0) - 1.3862944 * jax.random.uniform(key_of[2], (NT,), jnp.float32) ** steps_of(key_of[2], (NT,), ((0, 32),), -0.2, 0.2)), 0.5, 2.0)
    control_weight = jnp.clip(jnp.exp(jax.random.uniform(key_of[3], (NC,), jnp.float32, math.log(0.5), math.log(2.0))), 0.5, 2.0)
    band = draw_band(jax.random.fold_in(key_of[5], 71), 0)
    return {"treated": treated, "control": control, "treated_weight": treated_weight, "control_weight": control_weight, "band": band}


SMOOTHING_TEMP = 0.05
EPSILON = 1e-06

def normalize(features):
    values = features.astype(jnp.float32)
    return (values * lax.rsqrt(lax.optimization_barrier(jnp.mean(values * values, axis=1, keepdims=True)) + EPSILON)).astype(jnp.bfloat16)

def expand(pair_blocks, block_rows):
    block_count, column_count = pair_blocks.shape
    full = jnp.broadcast_to(pair_blocks[:, None, :, None], (block_count, block_rows, column_count, block_rows))
    return full.reshape(block_count * block_rows, column_count * block_rows)

def reference(treated, control, treated_weight, control_weight, band):
    wide_count = N_WIDE
    treated_norm = normalize(treated).reshape(wide_count, SLAB, REPRESENT_WIDTH)
    control_norm = normalize(control)
    slabs = control_norm.reshape(wide_count, SLAB, REPRESENT_WIDTH)
    zero_slab = jnp.zeros((1, SLAB, REPRESENT_WIDTH), jnp.bfloat16)
    padded = jnp.concatenate([zero_slab, slabs, zero_slab], axis=0)
    blocks = band.reshape(wide_count, SB, 3 * SB)
    weights_treated = treated_weight.reshape(wide_count, SLAB)
    indices = jnp.arange(wide_count, dtype=jnp.int32)
    zero_row = jnp.zeros((1, SLAB), jnp.float32)

    def kernel_of(slab_index):
        band_span = lax.dynamic_slice_in_dim(padded, slab_index, 3, 0).reshape(3 * SLAB, REPRESENT_WIDTH)
        pairwise_inner = jnp.dot(treated_norm[slab_index], band_span.T, preferred_element_type=jnp.float32)
        paired_mask = expand(blocks[slab_index], BLOCK) > 0
        return (band_span, jnp.where(paired_mask, jnp.exp(pairwise_inner / (REPRESENT_WIDTH * SMOOTHING_TEMP)), 0.0))
    col_pad = jnp.concatenate([zero_row, jnp.ones((wide_count, SLAB), jnp.float32), zero_row], axis=0)
    row_scale = jnp.zeros((wide_count, SLAB), jnp.float32)
    for sweep_index in range(SWEEPS):

        def sweep_part(slab_index, col_pad=col_pad):
            band_span, kernel = kernel_of(slab_index)
            scales = lax.dynamic_slice_in_dim(col_pad, slab_index, 3, 0).reshape(3 * SLAB)
            row_values = weights_treated[slab_index] / lax.optimization_barrier(jnp.sum(kernel * scales[None, :], axis=1))
            return (row_values, lax.optimization_barrier(jnp.sum(kernel * row_values[:, None], axis=0)).reshape(3, SLAB))
        row_scale, column_parts = lax.map(sweep_part, indices)
        column_total = jnp.zeros((wide_count + 2, SLAB), jnp.float32)
        column_total = column_total.at[0:wide_count].add(column_parts[:, 0])
        column_total = column_total.at[1:wide_count + 1].add(column_parts[:, 1])
        column_total = column_total.at[2:wide_count + 2].add(column_parts[:, 2])
        col_scale = control_weight.reshape(wide_count, SLAB) / column_total[1:wide_count + 1]
        col_pad = jnp.concatenate([zero_row, col_scale, zero_row], axis=0)

    def finish(pull_total, slab_index):
        band_span, kernel = kernel_of(slab_index)
        scales = lax.dynamic_slice_in_dim(col_pad, slab_index, 3, 0).reshape(3 * SLAB)
        transport = row_scale[slab_index][:, None] * kernel * scales[None, :]
        plan_bf = transport.astype(jnp.bfloat16)
        pulled = jnp.dot(plan_bf, band_span, preferred_element_type=jnp.float32)
        own_rows = treated_norm[slab_index]
        treated_grad = lax.optimization_barrier(jnp.sum(transport, axis=1))[:, None] * own_rows.astype(jnp.float32) - pulled
        pushed = jnp.dot(plan_bf.T, own_rows, preferred_element_type=jnp.float32).reshape(3, SLAB, REPRESENT_WIDTH)
        current = lax.dynamic_slice_in_dim(pull_total, slab_index, 3, 0)
        pull_total = lax.dynamic_update_slice_in_dim(pull_total, current + pushed, slab_index, 0)
        return (pull_total, treated_grad)
    pull_total, treated_grad = lax.scan(finish, jnp.zeros((wide_count + 2, SLAB, REPRESENT_WIDTH), jnp.float32), indices)
    grad_treated = treated_grad.reshape(NT, REPRESENT_WIDTH)
    grad_control = control_weight[:, None] * control_norm.astype(jnp.float32) - pull_total[1:wide_count + 1].reshape(NC, REPRESENT_WIDTH)
    return (grad_treated, grad_control)
```

```python
import functools

import jax
import jax.numpy as jnp
from jax import lax
from jax.experimental import pallas as pl
from jax.experimental.pallas import tpu as pltpu
from jax.sharding import PartitionSpec as P

SWEEPS = 2
SMOOTHING_TEMP = 0.05
EPSILON = 1e-06
LANES = 128
CHUNKS = 4
OWN, NEAR, FAR = 0, 1, 2
MESH = pl.DeviceIdType.MESH
F32 = jnp.float32
BF16 = jnp.bfloat16


def normalize(block):
    values = block.astype(F32)
    return (
        values * lax.rsqrt(jnp.mean(values * values, axis=1, keepdims=True) + EPSILON)
    ).astype(BF16)


def to_columns(row):
    return jnp.transpose(jnp.broadcast_to(row, (LANES, row.shape[1])))


def lane_sums(parts):
    return jnp.sum(jnp.transpose(parts), axis=0, keepdims=True)


def body(
    wide_size, narrow_size, scale,
    t_ref, c_ref, tw_ref, cw_ref, band_ref, gt_ref, gc_ref,
    tn, cn, kmat, plan, aux, aux_in, rs, rr, cs, cr,
    far_out, far_in, near_sum, near_out, near_in, own_pull,
    pair_out, pair_in, cross_out, cross_in,
    bulk_sem, relay_sem, aux_sem, row_sem, col_sem, far_sem, near_sem, pair_sem, cross_sem,
):
    w = lax.axis_index("wide")
    n = lax.axis_index("narrow")
    rows, features = t_ref.shape
    slab = c_ref.shape[0]
    blocks = slab // LANES
    block_rows = rows // band_ref.shape[0]
    step = 1 - 2 * (w % 2)
    near, far = w + step, w - step
    near2, far2 = w + 2 * step, w - 2 * step
    has_far = (far >= 0) & (far < wide_size)
    has_near2 = (near2 >= 0) & (near2 < wide_size)
    pair = n + 1 - 2 * (n % 2)
    cross = (n + 2) % narrow_size
    cross_pair = (pair + 2) % narrow_size

    def copy(src, dst, sems, index, wide, narrow):
        return pltpu.make_async_remote_copy(
            src_ref=src, dst_ref=dst,
            send_sem=sems.at[(0,) + index], recv_sem=sems.at[(1,) + index],
            device_id=(wide, narrow), device_id_type=MESH,
        )

    barrier = pltpu.get_barrier_semaphore()

    def greet(wide, narrow):
        pl.semaphore_signal(barrier, inc=1, device_id=(wide, narrow), device_id_type=MESH)

    greet(near, n)
    for other in range(1, narrow_size):
        greet(w, (n + other) % narrow_size)

    @pl.when(has_far)
    def _():
        greet(far, n)
        greet(far2, n)

    @pl.when(has_near2)
    def _():
        greet(near2, n)

    tn[OWN] = normalize(t_ref[...])
    for side in range(3):
        for block in range(blocks):
            k = side * blocks + block
            aux[side, 0:2, block * LANES:(block + 1) * LANES] = jnp.broadcast_to(
                band_ref[:, k:k + 1].astype(F32), (2, LANES)
            )
        aux[side, 2:3, 0:rows] = tw_ref[...]

    @pl.when(jnp.logical_not(has_far))
    def _():
        tn[FAR] = jnp.zeros((rows, features), BF16)
        aux_in[1] = jnp.zeros(aux_in.shape[1:], F32)
        for sweep in range(SWEEPS):
            rr[sweep, 2] = jnp.ones((1, rows), F32)
            rr[sweep, 3] = jnp.zeros((1, rows), F32)
            rr[sweep, 5] = jnp.zeros((1, rows), F32)

    @pl.when(jnp.logical_not(has_near2))
    def _():
        far_in[...] = jnp.zeros((rows, features), BF16)
        for sweep in range(SWEEPS):
            rr[sweep, 4] = jnp.zeros((1, rows), F32)

    pl.semaphore_wait(barrier, narrow_size + has_far.astype(jnp.int32) * 2 + has_near2.astype(jnp.int32))

    size = rows // CHUNKS
    part = [pl.ds(chunk * size, size) for chunk in range(CHUNKS)]
    aux_near = copy(aux.at[step + 1], aux_in.at[0], aux_sem, (0,), near, n)
    aux_far = copy(aux.at[1 - step], aux_in.at[1], aux_sem, (1,), far, n)
    bulk = [
        copy(tn.at[OWN, part[i]], tn.at[NEAR, part[i]], bulk_sem, (i,), near, n)
        for i in range(CHUNKS)
    ]
    relay = [
        copy(tn.at[NEAR, part[i]], tn.at[FAR, part[i]], relay_sem, (i,), near2, n)
        for i in range(CHUNKS)
    ]
    aux_near.start()

    @pl.when(has_far)
    def _():
        aux_far.start()

    for item in bulk:
        item.start()

    for quarter in range(narrow_size):
        at = pl.ds(quarter * (slab // narrow_size), slab // narrow_size)
        cn[at, :] = normalize(c_ref[at, :])

    def kernel_block(shard, mask_ref):
        sums = []
        for block in range(rows // block_rows):
            at = slice(block * block_rows, (block + 1) * block_rows)
            inner = lax.dot_general(
                tn[shard, at, :], cn[...], (((1,), (1,)), ((), ())), preferred_element_type=F32
            )
            entries = jnp.where(mask_ref[block:block + 1, :] > 0, jnp.exp(inner * scale), 0.0)
            kmat[shard, at, :] = entries
            total = entries[:, 0:LANES]
            for j in range(1, blocks):
                total = total + entries[:, j * LANES:(j + 1) * LANES]
            sums.append(total)
        return jnp.concatenate(sums, axis=0)

    slot_of = {NEAR: 0, OWN: 1, FAR: 2}
    rs[0, slot_of[OWN]] = lane_sums(kernel_block(OWN, aux.at[1]))

    for i in range(CHUNKS):
        bulk[i].wait_recv()

        @pl.when(has_near2)
        def _(i=i):
            relay[i].start()

    aux_near.wait_recv()
    rs[0, slot_of[NEAR]] = lane_sums(kernel_block(NEAR, aux_in.at[0]))

    @pl.when(has_far)
    def _():
        aux_far.wait_recv()
        for i in range(CHUNKS):
            relay[i].wait_recv()

    rs[0, slot_of[FAR]] = lane_sums(kernel_block(FAR, aux_in.at[1]))

    weights = {
        OWN: tw_ref[...],
        NEAR: aux_in[0, 2:3, 0:rows],
        FAR: aux_in[1, 2:3, 0:rows],
    }
    cols = [slice(j * LANES, (j + 1) * LANES) for j in range(blocks)]
    own_mass = cw_ref[pl.ds(w, 1), :]
    col_scale = None
    row_scale = None
    for sweep in range(SWEEPS):
        if sweep:
            for shard in (OWN, NEAR, FAR):
                total = kmat[shard, :, cols[0]] * col_scale[:, cols[0]]
                for j in range(1, blocks):
                    total = total + kmat[shard, :, cols[j]] * col_scale[:, cols[j]]
                rs[sweep, slot_of[shard]] = lane_sums(total)
        to_near = copy(rs.at[sweep, pl.ds(0, 2)], rr.at[sweep, pl.ds(0, 2)], row_sem, (sweep, 0), near, n)
        to_far = copy(rs.at[sweep, pl.ds(1, 2)], rr.at[sweep, pl.ds(2, 2)], row_sem, (sweep, 1), far, n)
        to_near2 = copy(rs.at[sweep, pl.ds(0, 1)], rr.at[sweep, pl.ds(5, 1)], row_sem, (sweep, 2), near2, n)
        to_far2 = copy(rs.at[sweep, pl.ds(2, 1)], rr.at[sweep, pl.ds(4, 1)], row_sem, (sweep, 3), far2, n)

        @pl.when(has_far)
        def _(to_far=to_far, to_far2=to_far2):
            to_far.start()
            to_far2.start()

        @pl.when(has_near2)
        def _(to_near2=to_near2):
            to_near2.start()

        to_near.start()
        to_near.wait_recv()

        @pl.when(has_far)
        def _(to_far=to_far, to_near2=to_near2):
            to_far.wait_recv()
            to_near2.wait_recv()

        @pl.when(has_near2)
        def _(to_far2=to_far2):
            to_far2.wait_recv()

        totals = {
            OWN: rs[sweep, 1] + rr[sweep, 0] + rr[sweep, 3],
            NEAR: rs[sweep, 0] + rr[sweep, 1] + rr[sweep, 4],
            FAR: rs[sweep, 2] + rr[sweep, 2] + rr[sweep, 5],
        }
        row_scale = {shard: to_columns(weights[shard] / totals[shard]) for shard in totals}
        for j in range(blocks):
            total = jnp.zeros((8, LANES), F32)
            for shard in (OWN, NEAR, FAR):
                total = total + jnp.sum(
                    (kmat[shard, :, cols[j]] * row_scale[shard]).reshape(rows // 8, 8, LANES), axis=0
                )
            cs[sweep, :, cols[j]] = jnp.sum(total, axis=0, keepdims=True)
        sends = [
            copy(cs.at[sweep], cr.at[sweep, other - 1], col_sem, (sweep, other - 1), w, (n + other) % narrow_size)
            for other in range(1, narrow_size)
        ]
        for item in sends:
            item.start()
        for item in sends:
            item.wait_recv()
        total = cs[sweep]
        for other in range(narrow_size - 1):
            total = total + cr[sweep, other]
        col_scale = own_mass / total

    def plan_block(shard):
        total = jnp.zeros((rows, LANES), F32)
        for j in range(blocks):
            value = kmat[shard, :, cols[j]] * row_scale[shard] * col_scale[:, cols[j]]
            total = total + value
            plan[shard, :, cols[j]] = value.astype(BF16)
        return jnp.sum(total, axis=1, keepdims=True)

    def pull(shard, mass):
        pulled = jnp.dot(plan[shard], cn[...], preferred_element_type=F32)
        return mass * tn[shard].astype(F32) - pulled

    far_out[...] = pull(FAR, plan_block(FAR)).astype(BF16)
    far_send = [
        copy(far_out.at[part[i]], far_in.at[part[i]], far_sem, (i,), far2, n) for i in range(CHUNKS)
    ]

    @pl.when(has_far)
    def _():
        for item in far_send:
            item.start()

    near_mass = plan_block(NEAR)
    own_mass_rows = plan_block(OWN)

    quarter_rows = slab // narrow_size

    def push(quarter):
        at = pl.ds(pl.multiple_of(quarter * quarter_rows, quarter_rows), quarter_rows)
        total = jnp.zeros((quarter_rows, features), F32)
        for shard in (OWN, NEAR, FAR):
            total = total + lax.dot_general(
                plan[shard, :, at], tn[shard], (((0,), (0,)), ((), ())), preferred_element_type=F32
            )
        return total

    pair_send = [copy(pair_out.at[i], pair_in.at[i], pair_sem, (i,), w, pair) for i in range(2)]
    pair_out[0] = push(cross_pair).astype(BF16)
    pair_send[0].start()
    near_sum[...] = pull(NEAR, near_mass)
    own_push = push(cross)
    pair_send[0].wait_recv()
    cross_out[...] = (own_push + pair_in[0].astype(F32)).astype(BF16)
    cross_send = copy(cross_out, cross_in, cross_sem, (0,), w, cross)
    cross_send.start()
    pair_out[1] = push(pair).astype(BF16)
    pair_send[1].start()

    near_send = [
        copy(near_out.at[part[i]], near_in.at[part[i]], near_sem, (i,), near, n) for i in range(CHUNKS)
    ]
    for i in range(CHUNKS):
        @pl.when(has_near2)
        def _(i=i):
            far_send[i].wait_recv()

        near_out[part[i], :] = (near_sum[part[i], :] + far_in[part[i], :].astype(F32)).astype(BF16)
        near_send[i].start()

    own_pull[...] = pull(OWN, own_mass_rows)
    at = pl.ds(pl.multiple_of(n * quarter_rows, quarter_rows), quarter_rows)
    mass = to_columns(cw_ref[pl.ds(w, 1), at])
    own_rows = cn[at, :].astype(F32)
    own_push = push(n)
    pair_send[1].wait_recv()
    own_push = own_push + pair_in[1].astype(F32)
    for j in range(features // LANES):
        lanes = slice(j * LANES, (j + 1) * LANES)
        gc_ref[:, lanes] = mass * own_rows[:, lanes] - own_push[:, lanes]
    cross_send.wait_recv()
    gc_ref[...] = gc_ref[...] - cross_in[...].astype(F32)
    for i in range(CHUNKS):
        near_send[i].wait_recv()
        gt_ref[part[i], :] = own_pull[part[i], :] + near_in[part[i], :].astype(F32)

    aux_near.wait_send()
    for item in bulk + near_send + pair_send + [cross_send]:
        item.wait_send()
    for sweep in range(SWEEPS):
        copy(rs.at[sweep, pl.ds(0, 2)], rr.at[sweep, pl.ds(0, 2)], row_sem, (sweep, 0), near, n).wait_send()
        for other in range(1, narrow_size):
            copy(
                cs.at[sweep], cr.at[sweep, other - 1], col_sem, (sweep, other - 1), w, (n + other) % narrow_size
            ).wait_send()

    @pl.when(has_far)
    def _():
        aux_far.wait_send()
        for item in far_send:
            item.wait_send()
        for sweep in range(SWEEPS):
            copy(rs.at[sweep, pl.ds(1, 2)], rr.at[sweep, pl.ds(2, 2)], row_sem, (sweep, 1), far, n).wait_send()
            copy(rs.at[sweep, pl.ds(2, 1)], rr.at[sweep, pl.ds(4, 1)], row_sem, (sweep, 3), far2, n).wait_send()

    @pl.when(has_near2)
    def _():
        for item in relay:
            item.wait_send()
        for sweep in range(SWEEPS):
            copy(rs.at[sweep, pl.ds(0, 1)], rr.at[sweep, pl.ds(5, 1)], row_sem, (sweep, 2), near2, n).wait_send()


def shards(wide_size, narrow_size, treated, control, treated_weight, control_weight, band):
    rows, features = treated.shape
    slab = control.shape[0]
    quarter = slab // narrow_size
    vmem = pl.BlockSpec(memory_space=pltpu.VMEM)
    dma = lambda *shape: pltpu.SemaphoreType.DMA((2,) + shape)
    block = pltpu.VMEM((rows, features), BF16)
    scratch = [
        pltpu.VMEM((3, rows, features), BF16),
        pltpu.VMEM((slab, features), BF16),
        pltpu.VMEM((3, rows, slab), F32),
        pltpu.VMEM((3, rows, slab), BF16),
        pltpu.VMEM((3, 4, slab), F32),
        pltpu.VMEM((2, 4, slab), F32),
        pltpu.VMEM((SWEEPS, 3, 1, rows), F32),
        pltpu.VMEM((SWEEPS, 6, 1, rows), F32),
        pltpu.VMEM((SWEEPS, 1, slab), F32),
        pltpu.VMEM((SWEEPS, narrow_size - 1, 1, slab), F32),
        block, block,
        pltpu.VMEM((rows, features), F32),
        block, block,
        pltpu.VMEM((rows, features), F32),
        pltpu.VMEM((2, quarter, features), BF16),
        pltpu.VMEM((2, quarter, features), BF16),
        pltpu.VMEM((quarter, features), BF16),
        pltpu.VMEM((quarter, features), BF16),
        dma(CHUNKS), dma(CHUNKS), dma(2), dma(SWEEPS, 4), dma(SWEEPS, narrow_size - 1),
        dma(CHUNKS), dma(CHUNKS), dma(2), dma(1),
    ]
    scale = 1.0 / (features * SMOOTHING_TEMP)
    return pl.pallas_call(
        functools.partial(body, wide_size, narrow_size, scale),
        out_shape=(
            jax.ShapeDtypeStruct((rows, features), F32),
            jax.ShapeDtypeStruct((quarter, features), F32),
        ),
        in_specs=[vmem] * 5,
        out_specs=(vmem, vmem),
        scratch_shapes=scratch,
        compiler_params=pltpu.CompilerParams(
            collective_id=0, has_side_effects=True, vmem_limit_bytes=40 * 1024 * 1024
        ),
    )(
        treated,
        control,
        treated_weight.reshape(1, rows),
        control_weight.reshape(wide_size, slab),
        band,
    )


def solution(mesh):
    return jax.shard_map(
        functools.partial(shards, mesh.shape["wide"], mesh.shape["narrow"]),
        mesh=mesh,
        in_specs=(
            P(("wide", "narrow"), None),
            P("wide", None),
            P(("wide", "narrow")),
            P(),
            P(("wide", "narrow"), None),
        ),
        out_specs=(P(("wide", "narrow"), None), P(("wide", "narrow"), None)),
        check_vma=False,
    )
```

```python
import functools

import jax
import jax.numpy as jnp
from jax import lax
from jax.experimental import pallas as pl
from jax.experimental.pallas import tpu as pltpu
from jax.sharding import PartitionSpec as P

SWEEPS = 2
SMOOTHING_TEMP = 0.05
EPSILON = 1e-06
LANES = 128
CHUNKS = 8
OWN, NEAR, FAR = 0, 1, 2
MESH = pl.DeviceIdType.MESH
F32 = jnp.float32
BF16 = jnp.bfloat16


def normalize(block):
    values = block.astype(F32)
    return (
        values * lax.rsqrt(jnp.mean(values * values, axis=1, keepdims=True) + EPSILON)
    ).astype(BF16)


def to_columns(row):
    return jnp.transpose(jnp.broadcast_to(row, (LANES, row.shape[1])))


def lane_sums(parts):
    return jnp.sum(jnp.transpose(parts), axis=0, keepdims=True)


def body(
    wide_size, narrow_size, scale,
    t_ref, c_ref, tw_ref, cw_ref, band_ref, gt_ref, gc_ref,
    t_in, c_in, cw_in, own_cw, tn, cn, kmat, plan, aux, aux_in, rs, rr, cs, cr,
    far_out, far_in, near_sum, near_out, near_in, own_pull,
    pair_out, pair_in, cross_out, cross_in,
    bulk_sem, relay_sem, aux_sem, row_sem, col_sem, far_sem, near_sem, pair_sem, cross_sem, load_sem,
):
    w = lax.axis_index("wide")
    n = lax.axis_index("narrow")
    rows, features = t_ref.shape
    slab = c_ref.shape[0]
    blocks = slab // LANES
    block_rows = rows // band_ref.shape[0]
    step = 1 - 2 * (w % 2)
    near, far = w + step, w - step
    near2, far2 = w + 2 * step, w - 2 * step
    has_far = (far >= 0) & (far < wide_size)
    has_near2 = (near2 >= 0) & (near2 < wide_size)
    pair = n + 1 - 2 * (n % 2)
    cross = (n + 2) % narrow_size
    cross_pair = (pair + 2) % narrow_size

    def copy(src, dst, sems, index, wide, narrow):
        return pltpu.make_async_remote_copy(
            src_ref=src, dst_ref=dst,
            send_sem=sems.at[(0,) + index], recv_sem=sems.at[(1,) + index],
            device_id=(wide, narrow), device_id_type=MESH,
        )

    loads = [
        pltpu.make_async_copy(t_ref, t_in, load_sem.at[0]),
        pltpu.make_async_copy(cw_ref.at[pl.ds(pl.multiple_of(w * slab, slab), slab)], cw_in, load_sem.at[1]),
    ]
    pieces = [pl.ds(i * (slab // narrow_size), slab // narrow_size) for i in range(narrow_size)]
    loads += [
        pltpu.make_async_copy(c_ref.at[at], c_in.at[at], load_sem.at[2 + i]) for i, at in enumerate(pieces)
    ]
    for item in loads:
        item.start()

    barrier = pltpu.get_barrier_semaphore()

    def greet(wide, narrow):
        pl.semaphore_signal(barrier, inc=1, device_id=(wide, narrow), device_id_type=MESH)

    greet(near, n)
    for other in range(1, narrow_size):
        greet(w, (n + other) % narrow_size)

    @pl.when(has_far)
    def _():
        greet(far, n)
        greet(far2, n)

    @pl.when(has_near2)
    def _():
        greet(near2, n)

    for side in range(3):
        for block in range(blocks):
            k = side * blocks + block
            aux[side, 0:2, block * LANES:(block + 1) * LANES] = jnp.broadcast_to(
                band_ref[:, k:k + 1].astype(F32), (2, LANES)
            )
        aux[side, 2:3, 0:rows] = tw_ref[...]

    loads[0].wait()
    tn[OWN] = normalize(t_in[...])

    @pl.when(jnp.logical_not(has_far))
    def _():
        tn[FAR] = jnp.zeros((rows, features), BF16)
        aux_in[1] = jnp.zeros(aux_in.shape[1:], F32)
        for sweep in range(SWEEPS):
            rr[sweep, 2] = jnp.ones((1, rows), F32)
            rr[sweep, 3] = jnp.zeros((1, rows), F32)
            rr[sweep, 5] = jnp.zeros((1, rows), F32)

    @pl.when(jnp.logical_not(has_near2))
    def _():
        far_in[...] = jnp.zeros((rows, features), BF16)
        for sweep in range(SWEEPS):
            rr[sweep, 4] = jnp.zeros((1, rows), F32)

    pl.semaphore_wait(barrier, narrow_size + has_far.astype(jnp.int32) * 2 + has_near2.astype(jnp.int32))

    size = rows // CHUNKS
    part = [pl.ds(chunk * size, size) for chunk in range(CHUNKS)]
    aux_near = copy(aux.at[step + 1], aux_in.at[0], aux_sem, (0,), near, n)
    aux_far = copy(aux.at[1 - step], aux_in.at[1], aux_sem, (1,), far, n)
    bulk = [
        copy(tn.at[OWN, part[i]], tn.at[NEAR, part[i]], bulk_sem, (i,), near, n)
        for i in range(CHUNKS)
    ]
    relay = [
        copy(tn.at[NEAR, part[i]], tn.at[FAR, part[i]], relay_sem, (i,), near2, n)
        for i in range(CHUNKS)
    ]
    aux_near.start()

    @pl.when(has_far)
    def _():
        aux_far.start()

    for item in bulk:
        item.start()

    for i, at in enumerate(pieces):
        loads[2 + i].wait()
        cn[at, :] = normalize(c_in[at, :])
    loads[1].wait()
    own_cw[...] = cw_in[...].reshape(1, slab)

    def kernel_block(shard, mask_ref, block):
        at = slice(block * block_rows, (block + 1) * block_rows)
        inner = lax.dot_general(
            tn[shard, at, :], cn[...], (((1,), (1,)), ((), ())), preferred_element_type=F32
        )
        entries = jnp.where(mask_ref[block:block + 1, :] > 0, jnp.exp(inner * scale), 0.0)
        kmat[shard, at, :] = entries
        total = entries[:, 0:LANES]
        for j in range(1, blocks):
            total = total + entries[:, j * LANES:(j + 1) * LANES]
        rs[0, slot_of[shard], :, at] = lane_sums(total)

    slot_of = {NEAR: 0, OWN: 1, FAR: 2}
    per_block = CHUNKS * block_rows // rows

    def pass_on(i):
        bulk[i].wait_recv()

        @pl.when(has_near2)
        def _():
            relay[i].start()

    blocks_of_rows = rows // block_rows
    for block in range(blocks_of_rows):
        pass_on(block)
        kernel_block(OWN, aux.at[1], block)
    for i in range(blocks_of_rows, CHUNKS):
        pass_on(i)
    aux_near.wait_recv()
    for block in range(blocks_of_rows):
        kernel_block(NEAR, aux_in.at[0], block)
    for block in range(blocks_of_rows):
        @pl.when(has_far)
        def _(block=block):
            if block == 0:
                aux_far.wait_recv()
            for i in range(block * per_block, (block + 1) * per_block):
                relay[i].wait_recv()

        kernel_block(FAR, aux_in.at[1], block)

    weights = {
        OWN: tw_ref[...],
        NEAR: aux_in[0, 2:3, 0:rows],
        FAR: aux_in[1, 2:3, 0:rows],
    }
    cols = [slice(j * LANES, (j + 1) * LANES) for j in range(blocks)]
    own_mass = own_cw[...]
    col_scale = None
    row_scale = None
    for sweep in range(SWEEPS):
        if sweep:
            for shard in (OWN, NEAR, FAR):
                total = kmat[shard, :, cols[0]] * col_scale[:, cols[0]]
                for j in range(1, blocks):
                    total = total + kmat[shard, :, cols[j]] * col_scale[:, cols[j]]
                rs[sweep, slot_of[shard]] = lane_sums(total)
        to_near = copy(rs.at[sweep, pl.ds(0, 2)], rr.at[sweep, pl.ds(0, 2)], row_sem, (sweep, 0), near, n)
        to_far = copy(rs.at[sweep, pl.ds(1, 2)], rr.at[sweep, pl.ds(2, 2)], row_sem, (sweep, 1), far, n)
        to_near2 = copy(rs.at[sweep, pl.ds(0, 1)], rr.at[sweep, pl.ds(5, 1)], row_sem, (sweep, 2), near2, n)
        to_far2 = copy(rs.at[sweep, pl.ds(2, 1)], rr.at[sweep, pl.ds(4, 1)], row_sem, (sweep, 3), far2, n)

        @pl.when(has_far)
        def _(to_far=to_far, to_far2=to_far2):
            to_far.start()
            to_far2.start()

        @pl.when(has_near2)
        def _(to_near2=to_near2):
            to_near2.start()

        to_near.start()
        to_near.wait_recv()

        @pl.when(has_far)
        def _(to_far=to_far, to_near2=to_near2):
            to_far.wait_recv()
            to_near2.wait_recv()

        @pl.when(has_near2)
        def _(to_far2=to_far2):
            to_far2.wait_recv()

        totals = {
            OWN: rs[sweep, 1] + rr[sweep, 0] + rr[sweep, 3],
            NEAR: rs[sweep, 0] + rr[sweep, 1] + rr[sweep, 4],
            FAR: rs[sweep, 2] + rr[sweep, 2] + rr[sweep, 5],
        }
        row_scale = {shard: to_columns(weights[shard] / totals[shard]) for shard in totals}
        for j in range(blocks):
            total = jnp.zeros((8, LANES), F32)
            for shard in (OWN, NEAR, FAR):
                total = total + jnp.sum(
                    (kmat[shard, :, cols[j]] * row_scale[shard]).reshape(rows // 8, 8, LANES), axis=0
                )
            cs[sweep, :, cols[j]] = jnp.sum(total, axis=0, keepdims=True)
        sends = [
            copy(cs.at[sweep], cr.at[sweep, other - 1], col_sem, (sweep, other - 1), w, (n + other) % narrow_size)
            for other in range(1, narrow_size)
        ]
        for item in sends:
            item.start()
        for item in sends:
            item.wait_recv()
        total = cs[sweep]
        for other in range(narrow_size - 1):
            total = total + cr[sweep, other]
        col_scale = own_mass / total

    def plan_block(shard):
        total = jnp.zeros((rows, LANES), F32)
        for j in range(blocks):
            value = kmat[shard, :, cols[j]] * row_scale[shard] * col_scale[:, cols[j]]
            total = total + value
            plan[shard, :, cols[j]] = value.astype(BF16)
        return jnp.sum(total, axis=1, keepdims=True)

    def pull(shard, mass):
        pulled = jnp.dot(plan[shard], cn[...], preferred_element_type=F32)
        return mass * tn[shard].astype(F32) - pulled

    far_out[...] = pull(FAR, plan_block(FAR)).astype(BF16)
    far_send = [
        copy(far_out.at[part[i]], far_in.at[part[i]], far_sem, (i,), far2, n) for i in range(CHUNKS)
    ]

    @pl.when(has_far)
    def _():
        for item in far_send:
            item.start()

    near_mass = plan_block(NEAR)
    own_mass_rows = plan_block(OWN)

    quarter_rows = slab // narrow_size

    def push(quarter):
        at = pl.ds(pl.multiple_of(quarter * quarter_rows, quarter_rows), quarter_rows)
        total = jnp.zeros((quarter_rows, features), F32)
        for shard in (OWN, NEAR, FAR):
            total = total + lax.dot_general(
                plan[shard, :, at], tn[shard], (((0,), (0,)), ((), ())), preferred_element_type=F32
            )
        return total

    near_send = [
        copy(near_out.at[part[i]], near_in.at[part[i]], near_sem, (i,), near, n) for i in range(CHUNKS)
    ]

    def pass_near(first, last):
        for i in range(first, last):
            @pl.when(has_near2)
            def _(i=i):
                far_send[i].wait_recv()

            near_out[part[i], :] = (near_sum[part[i], :] + far_in[part[i], :].astype(F32)).astype(BF16)
            near_send[i].start()

    pair_send = [copy(pair_out.at[i], pair_in.at[i], pair_sem, (i,), w, pair) for i in range(2)]
    pair_out[0] = push(cross_pair).astype(BF16)
    pair_send[0].start()
    near_sum[...] = pull(NEAR, near_mass)
    pass_near(0, 2)
    own_push = push(cross)
    pair_send[0].wait_recv()
    cross_out[...] = (own_push + pair_in[0].astype(F32)).astype(BF16)
    cross_send = copy(cross_out, cross_in, cross_sem, (0,), w, cross)
    cross_send.start()
    pass_near(2, 5)
    pair_out[1] = push(pair).astype(BF16)
    pair_send[1].start()

    pass_near(5, CHUNKS)

    own_pull[...] = pull(OWN, own_mass_rows)
    at = pl.ds(pl.multiple_of(n * quarter_rows, quarter_rows), quarter_rows)
    mass = to_columns(own_cw[:, at])
    own_rows = cn[at, :].astype(F32)
    own_push = push(n)
    pair_send[1].wait_recv()
    own_push = own_push + pair_in[1].astype(F32)
    for j in range(features // LANES):
        lanes = slice(j * LANES, (j + 1) * LANES)
        gc_ref[:, lanes] = mass * own_rows[:, lanes] - own_push[:, lanes]
    cross_send.wait_recv()
    gc_ref[...] = gc_ref[...] - cross_in[...].astype(F32)
    for i in range(CHUNKS):
        near_send[i].wait_recv()
        gt_ref[part[i], :] = own_pull[part[i], :] + near_in[part[i], :].astype(F32)

    aux_near.wait_send()
    for item in bulk + near_send + pair_send + [cross_send]:
        item.wait_send()
    for sweep in range(SWEEPS):
        copy(rs.at[sweep, pl.ds(0, 2)], rr.at[sweep, pl.ds(0, 2)], row_sem, (sweep, 0), near, n).wait_send()
        for other in range(1, narrow_size):
            copy(
                cs.at[sweep], cr.at[sweep, other - 1], col_sem, (sweep, other - 1), w, (n + other) % narrow_size
            ).wait_send()

    @pl.when(has_far)
    def _():
        aux_far.wait_send()
        for item in far_send:
            item.wait_send()
        for sweep in range(SWEEPS):
            copy(rs.at[sweep, pl.ds(1, 2)], rr.at[sweep, pl.ds(2, 2)], row_sem, (sweep, 1), far, n).wait_send()
            copy(rs.at[sweep, pl.ds(2, 1)], rr.at[sweep, pl.ds(4, 1)], row_sem, (sweep, 3), far2, n).wait_send()

    @pl.when(has_near2)
    def _():
        for item in relay:
            item.wait_send()
        for sweep in range(SWEEPS):
            copy(rs.at[sweep, pl.ds(0, 1)], rr.at[sweep, pl.ds(5, 1)], row_sem, (sweep, 2), near2, n).wait_send()


def shards(wide_size, narrow_size, treated, control, treated_weight, control_weight, band):
    rows, features = treated.shape
    slab = control.shape[0]
    quarter = slab // narrow_size
    hbm = pl.BlockSpec(memory_space=pl.ANY)
    vmem = pl.BlockSpec(memory_space=pltpu.VMEM)
    dma = lambda *shape: pltpu.SemaphoreType.DMA((2,) + shape)
    block = pltpu.VMEM((rows, features), BF16)
    scratch = [
        pltpu.VMEM((rows, features), BF16),
        pltpu.VMEM((slab, features), BF16),
        pltpu.VMEM((slab,), F32),
        pltpu.VMEM((1, slab), F32),
        pltpu.VMEM((3, rows, features), BF16),
        pltpu.VMEM((slab, features), BF16),
        pltpu.VMEM((3, rows, slab), F32),
        pltpu.VMEM((3, rows, slab), BF16),
        pltpu.VMEM((3, 4, slab), F32),
        pltpu.VMEM((2, 4, slab), F32),
        pltpu.VMEM((SWEEPS, 3, 1, rows), F32),
        pltpu.VMEM((SWEEPS, 6, 1, rows), F32),
        pltpu.VMEM((SWEEPS, 1, slab), F32),
        pltpu.VMEM((SWEEPS, narrow_size - 1, 1, slab), F32),
        block, block,
        pltpu.VMEM((rows, features), F32),
        block, block,
        pltpu.VMEM((rows, features), F32),
        pltpu.VMEM((2, quarter, features), BF16),
        pltpu.VMEM((2, quarter, features), BF16),
        pltpu.VMEM((quarter, features), BF16),
        pltpu.VMEM((quarter, features), BF16),
        dma(CHUNKS), dma(CHUNKS), dma(2), dma(SWEEPS, 4), dma(SWEEPS, narrow_size - 1),
        dma(CHUNKS), dma(CHUNKS), dma(2), dma(1),
        pltpu.SemaphoreType.DMA((2 + narrow_size,)),
    ]
    scale = 1.0 / (features * SMOOTHING_TEMP)
    outputs = pl.pallas_call(
        functools.partial(body, wide_size, narrow_size, scale),
        out_shape=(
            jax.ShapeDtypeStruct((rows, features), F32),
            jax.ShapeDtypeStruct((quarter, features), F32),
        ),
        in_specs=[hbm, hbm, vmem, hbm, vmem],
        out_specs=(vmem, vmem),
        scratch_shapes=scratch,
        compiler_params=pltpu.CompilerParams(
            collective_id=0, has_side_effects=True, vmem_limit_bytes=60 * 1024 * 1024
        ),
    )(
        treated,
        control,
        treated_weight.reshape(1, rows),
        control_weight,
        band,
    )
    def store_body(a, b, c, d):
        c[...] = a[...]
        d[...] = b[...]
    return pl.pallas_call(
        store_body,
        out_shape=tuple(jax.ShapeDtypeStruct(out.shape, out.dtype) for out in outputs),
        in_specs=[vmem] * 2,
        out_specs=(vmem, vmem),
    )(*outputs)


def solution(mesh):
    return jax.shard_map(
        functools.partial(shards, mesh.shape["wide"], mesh.shape["narrow"]),
        mesh=mesh,
        in_specs=(
            P(("wide", "narrow"), None),
            P("wide", None),
            P(("wide", "narrow")),
            P(),
            P(("wide", "narrow"), None),
        ),
        out_specs=(P(("wide", "narrow"), None), P(("wide", "narrow"), None)),
        check_vma=False,
    )
```
